32 devices in a mesh: groups: 2 (over x), blk: 16 (over z, y, core).
Axes of the slice: x: 2, y: 2, z: 4, core: 2. Of those that a mesh axis runs over, the one named last changes fastest.
Arguments:
- walkers: bfloat16 [192, 256, 128], P(('groups', 'blk')), parts along dimension 0, may hold values from -6 to 6
- inv_intersection: bfloat16 [192, 128, 128], P(('groups', 'blk')), parts along dimension 0, may hold values from -0.5 to 0.5
- trial_orbs: bfloat16 [256, 128], replicated, may hold values from -0.375 to 0.375
- cholesky: bfloat16 [4096, 256, 256], P(('groups', 'blk')), parts along dimension 0, may hold values from -0.02734375 to 0.02734375
- aux_fields: float32 [192, 2048], P('groups', 'blk'), parts along dimension 0, may hold values from -6 to 6
Outputs:
- new_walkers: bfloat16 [192, 256, 128], P(('groups', 'blk')), parts along dimension 0
- intersection: float32 [192, 128, 128], P(('groups', 'blk')), parts along dimension 0
The draws below stay inside these ranges and needn't reach their ends.
There are 2 independent parts, one for each index of `groups`. The reference program is written for one: setup_inputs(seed, part) draws one part's arguments, and reference() takes and returns one part's arrays. A program takes and returns all parts, laid end to end along the dimension named above; an argument that names none is the same for every part. Nothing has to cross between parts.
All inputs are finite; a program needn't handle non-finite values.
Results may differ from the reference program's by a relative error of at most 0.018.
Values may be sent and summed in bfloat16 or wider, within the bound.
A program may use at most 192 MiB of HBM per device.

```python
import jax
import jax.numpy as jnp
from jax import lax

NORB = 256
NOCC = 128
CH_DEV = 128
NCHOL = 2048
WALKERS = 96
N_BLK = 16


def raised(drawn, key, source, target, shards_of, factor):
    owner, partner = [(jnp.arange(drawn.shape[axis_at]) // (drawn.shape[axis_at] // shards_of)).reshape([-1 if axis == axis_at else 1 for axis in range(drawn.ndim)]) for axis_at in (source, target)]
    chosen = jax.random.permutation(key, shards_of)[partner]
    strong = (owner == chosen) | (owner == (partner + shards_of // 2) % shards_of)
    return jnp.where(strong, factor * drawn, drawn)


def block_levels(stream_key, extent, shards, least, high):
    factor_of, own = 1.0, jax.random.fold_in(stream_key, 6)
    for dim, shards_of in shards:
        heights = jnp.exp(jax.random.uniform(jax.random.fold_in(own, dim), (shards_of,), jnp.float32, least / len(shards), high / len(shards)))
        factor_of = factor_of * jnp.repeat(heights, extent[dim] // shards_of).reshape([-1 if axis == dim else 1 for axis in range(len(extent))])
    return factor_of


def scatter_about(key, dims, deviation, bound, cuts=(), dtype=jnp.bfloat16):
    factor_of = block_levels(key, dims, cuts, -0.22, 0.18) if cuts else 1.0
    values = jax.random.normal(key, dims, jnp.float32) * deviation * factor_of
    return jnp.minimum(jnp.maximum(values, -bound), bound).astype(dtype)


def heavy_noise(rng, dims, spread, reach, shards, heavy, dtype=jnp.bfloat16):
    result = spread * jax.random.normal(rng, dims, jnp.float32)
    if shards:
        result = result * block_levels(rng, dims, shards, -0.22, 0.18)
    return jnp.clip(raised(result, jax.random.fold_in(rng, 3), *heavy), -reach, reach).astype(dtype)


def setup_inputs(seed: int = 0, part: int = 0) -> dict:
    splits = jax.random.split(jax.random.key(seed), 6)
    part_keys = jax.random.split(jax.random.fold_in(splits[5], part), 6)
    walkers = scatter_about(part_keys[0], (WALKERS, NORB, NOCC), 1.0, 6.0, ((0, 16),))
    inv_intersection = scatter_about(part_keys[1], (WALKERS, NOCC, NOCC), NOCC ** -0.5, 0.5, ((0, 16),))
    trial_orbs = scatter_about(splits[2], (NORB, NOCC), NORB ** -0.5, 0.375)
    cholesky = scatter_about(part_keys[3], (NCHOL, NORB, NORB), (NCHOL * NORB // 12) ** -0.5, 0.02734375, ((0, 16),))
    aux_fields = heavy_noise(part_keys[4], (WALKERS, NCHOL), 1.0, 6.0, ((1, 16),), (1, 0, 16, 2.0), jnp.float32)
    return dict(walkers=walkers, inv_intersection=inv_intersection, trial_orbs=trial_orbs, cholesky=cholesky, aux_fields=aux_fields)


root_step = 0.1
bias_step = 0.5


def reference(walkers, inv_intersection, trial_orbs, cholesky, aux_fields):
    f32 = jnp.float32
    rotated = jnp.einsum('wpi,wij->wpj', walkers.astype(f32), inv_intersection.astype(f32)).astype(jnp.bfloat16)
    rotated_wide = rotated.astype(f32)
    trial_wide = trial_orbs.astype(f32)
    blocks = cholesky.reshape(N_BLK, CH_DEV, NORB, NORB)

    def bias_block(carry, chol_block):
        half_rot = jnp.einsum('pi,gpq->giq', trial_wide, chol_block.astype(f32)).astype(jnp.bfloat16)
        columns = jnp.einsum('giq,wqi->wg', half_rot.astype(f32), rotated_wide)
        return carry, columns

    unused, bias_blocks = lax.scan(bias_block, jnp.zeros((), f32), blocks)
    force_bias = jnp.transpose(bias_blocks, (1, 0, 2)).reshape(WALKERS, NCHOL)
    shifted = (aux_fields + bias_step * force_bias).astype(jnp.bfloat16)
    shifted_blocks = jnp.transpose(shifted.reshape(WALKERS, N_BLK, CH_DEV), (1, 0, 2))

    def potential_block(total, pieces):
        chol_block, field_block = pieces
        partial_value = jnp.einsum('wg,gpq->wpq', field_block.astype(f32), chol_block.astype(f32)).astype(jnp.bfloat16)
        return total + partial_value.astype(f32), jnp.zeros((), f32)

    summed_pot, unused2 = lax.scan(potential_block, jnp.zeros((WALKERS, NORB, NORB), f32), (blocks, shifted_blocks))
    potential = (root_step * summed_pot).astype(jnp.bfloat16)
    taylor_term = walkers
    summed = walkers.astype(f32)
    for degree in range(1, 5):
        product = jnp.einsum('wpq,wqi->wpi', potential.astype(f32), taylor_term.astype(f32))
        taylor_term = (product / degree).astype(jnp.bfloat16)
        summed = summed + taylor_term.astype(f32)
    new_walkers = summed.astype(jnp.bfloat16)
    intersection = jnp.einsum('pi,wpj->wij', trial_wide, new_walkers.astype(f32))
    return new_walkers, intersection
```

```python
import functools

import jax
import jax.numpy as jnp
import numpy as np
from jax import lax
from jax.experimental import pallas as pl
from jax.experimental.pallas import tpu as pltpu
from jax.sharding import PartitionSpec as P

root_step = 0.1
bias_step = 0.5
MESH = pl.DeviceIdType.MESH
bf16 = jnp.bfloat16
f32 = jnp.float32


def row_orders(planes):
    half = planes * 12
    order = np.zeros((2, 2, half), np.int64)
    for parity in range(2):
        for y in range(2):
            for m in range(half):
                if m < planes * 8:
                    dest, within = m // 8, m % 8
                else:
                    rest = m - planes * 8
                    side = (rest % 8) // 4
                    dest = 2 * (rest // 8) + (side if parity == 0 else 1 - side)
                    within = 8 + rest % 4
                order[parity, y, m] = (dest * 2 + y) * 12 + within
    return order.reshape(-1)[:, None] == np.arange(2 * half)[None, :]


def scatter_kernel(planes, chunks, s_ref, perm_ref, chol_ref, out_ref,
                   sib_s, sp, chol2, ysend, held, up, down,
                   s_sem, load_sem, chol_send, chol_recv, y_send, y_recv,
                   up_send, up_recv, down_send, down_recv, out_send, out_recv):
    norb, own_g, _ = chol_ref.shape
    span = norb // chunks
    rows = span * 12
    half = planes * 12
    me = lax.axis_index("blk")
    core = lax.rem(me, 2)
    y = lax.rem(lax.div(me, 2), 2)
    z = lax.div(me, 4)
    sibling = me + 1 - 2 * core
    across = me + 2 - 4 * y
    above = me + 4
    below = me - 4
    not_first, not_last = z > 0, z < planes - 1

    barrier = pltpu.get_barrier_semaphore()
    pl.semaphore_signal(barrier, inc=1, device_id={"blk": sibling}, device_id_type=MESH)
    pl.semaphore_signal(barrier, inc=1, device_id={"blk": across}, device_id_type=MESH)

    @pl.when(not_first)
    def _():
        pl.semaphore_signal(barrier, inc=1, device_id={"blk": below}, device_id_type=MESH)

    @pl.when(not_last)
    def _():
        pl.semaphore_signal(barrier, inc=1, device_id={"blk": above}, device_id_type=MESH)

    peers = 2 + jnp.where(not_first, 1, 0) + jnp.where(not_last, 1, 0)
    pl.semaphore_wait(barrier, peers)

    def remote(src, dst, send, recv, target):
        return pltpu.make_async_remote_copy(
            src_ref=src, dst_ref=dst, send_sem=send, recv_sem=recv,
            device_id={"blk": target}, device_id_type=MESH)

    def chol_load(k):
        return pltpu.make_async_copy(
            chol_ref.at[pl.ds(k * span, span), :, pl.ds(pl.multiple_of(core * 128, 128), 128)],
            chol2.at[pl.ds(k * span, span), pl.ds(0, own_g)], load_sem.at[k])

    def chol_swap(k):
        return remote(
            chol_ref.at[pl.ds(k * span, span), :, pl.ds(pl.multiple_of((1 - core) * 128, 128), 128)],
            chol2.at[pl.ds(k * span, span), pl.ds(own_g, own_g)],
            chol_send.at[k], chol_recv.at[k], sibling)

    def y_copy(k):
        return remote(ysend.at[k], held.at[k], y_send.at[k], y_recv.at[k], across)

    def out_copy(k):
        piece = out_ref.at[core, pl.ds(pl.multiple_of(k * rows, 16), rows)]
        return remote(piece, piece, out_send.at[k], out_recv.at[k], sibling)

    s_copy = remote(s_ref, sib_s, s_sem.at[0], s_sem.at[1], sibling)
    s_copy.start()

    def begin(k, carry):
        chol_load(k).start()
        chol_swap(k).start()
        return carry

    lax.fori_loop(0, chunks, begin, 0)
    s_copy.wait()
    for parity in range(2):
        for side in range(2):
            pick = perm_ref[pl.ds((parity * 2 + side) * half, half), :]
            sp[parity, side, :, 0:own_g] = jnp.dot(
                pick, s_ref[...], preferred_element_type=f32).astype(bf16)
            sp[parity, side, :, own_g:] = jnp.dot(
                pick, sib_s[...], preferred_element_type=f32).astype(bf16)

    low = lax.broadcasted_iota(jnp.int32, (8, 128), 0) < 4

    def products(k, side, dst, add):
        def quad(j, carry):
            first = k * span + j * 4
            r = [jnp.dot(sp[i % 2, side], chol2[first + i], preferred_element_type=f32)
                 for i in range(4)]
            at = pl.ds(pl.multiple_of(j * 48, 48), 48)
            for d in range(planes):
                pieces = []
                mixed = slice(planes * 8 + (d // 2) * 8, planes * 8 + (d // 2) * 8 + 8)
                for i in (0, 2):
                    even, odd = r[i][mixed], r[i + 1][mixed]
                    pieces += [r[i][d * 8:d * 8 + 8], r[i + 1][d * 8:d * 8 + 8],
                               jnp.where(low, even, odd) if d % 2 == 0 else jnp.where(low, odd, even)]
                value = jnp.concatenate(pieces, axis=0)
                if add:
                    value = value + dst[k, d, at].astype(f32)
                dst[k, d, at] = value.astype(bf16)
            return carry

        lax.fori_loop(0, span // 4, quad, 0)

    def hop(k, d, buf, send, recv, has_source, target):
        @pl.when(has_source)
        def _():
            remote(buf.at[k, d], buf.at[k, d], send.at[k, d], recv.at[k, d], target).wait_recv()
            buf[k, d] = (buf[k, d].astype(f32) + held[k, d].astype(f32)).astype(bf16)
            remote(buf.at[k, d], buf.at[k, d], send.at[k, d], recv.at[k, d], target).start()

        @pl.when(jnp.logical_not(has_source))
        def _():
            remote(held.at[k, d], buf.at[k, d], send.at[k, d], recv.at[k, d], target).start()

    def step(t, carry):
        @pl.when(t < chunks)
        def _():
            chol_load(t).wait()
            chol_swap(t).wait_recv()
            products(t, 1 - y, ysend, False)
            y_copy(t).start()

        @pl.when(jnp.logical_and(t >= 1, t <= chunks))
        def _():
            k = t - 1
            y_copy(k).wait_recv()
            products(k, y, held, True)

        ku = t - 1 - z

        @pl.when(jnp.logical_and(ku >= 0, ku < chunks))
        def _():
            for d in range(1, planes):
                @pl.when(d > z)
                def _():
                    hop(ku, d, up, up_send, up_recv, not_first, above)

        kd = t - planes + z

        @pl.when(jnp.logical_and(kd >= 0, kd < chunks))
        def _():
            for d in range(planes - 1):
                @pl.when(d < z)
                def _():
                    hop(kd, d, down, down_send, down_recv, not_last, below)

        kf = t - planes

        @pl.when(jnp.logical_and(kf >= 0, kf < chunks))
        def _():
            at = pl.ds(pl.multiple_of(kf * rows, 16), rows)

            @pl.when(jnp.logical_not(not_first))
            def _():
                remote(down.at[kf, z], down.at[kf, z], down_send.at[kf, z], down_recv.at[kf, z], above).wait_recv()
                out_ref[core, at] = (held[kf, z].astype(f32) + down[kf, z].astype(f32)).astype(bf16)

            @pl.when(jnp.logical_not(not_last))
            def _():
                remote(up.at[kf, z], up.at[kf, z], up_send.at[kf, z], up_recv.at[kf, z], below).wait_recv()
                out_ref[core, at] = (held[kf, z].astype(f32) + up[kf, z].astype(f32)).astype(bf16)

            @pl.when(jnp.logical_and(not_first, not_last))
            def _():
                remote(down.at[kf, z], down.at[kf, z], down_send.at[kf, z], down_recv.at[kf, z], above).wait_recv()
                remote(up.at[kf, z], up.at[kf, z], up_send.at[kf, z], up_recv.at[kf, z], below).wait_recv()
                out_ref[core, at] = (
                    held[kf, z].astype(f32) + up[kf, z].astype(f32) + down[kf, z].astype(f32)
                ).astype(bf16)

            out_copy(kf).start()

        return carry

    lax.fori_loop(0, chunks + planes, step, 0)

    def finish(k, carry):
        chol_swap(k).wait_send()
        y_copy(k).wait_send()
        for d in range(planes):
            @pl.when(d > z)
            def _():
                remote(up.at[k, d], up.at[k, d], up_send.at[k, d], up_recv.at[k, d], above).wait_send()

            @pl.when(d < z)
            def _():
                remote(down.at[k, d], down.at[k, d], down_send.at[k, d], down_recv.at[k, d], below).wait_send()

        out_copy(k).wait_send()
        other = out_ref.at[1 - core, pl.ds(pl.multiple_of(k * rows, 16), rows)]
        remote(other, other, out_send.at[k], out_recv.at[k], sibling).wait_recv()
        return carry

    lax.fori_loop(0, chunks, finish, 0)


def reduced_potential(shifted, chol_t, planes, chunks=16):
    n_walkers, own_g = shifted.shape
    norb = chol_t.shape[0]
    rows = norb // chunks * 12
    slots = pltpu.VMEM((chunks, planes, rows, 128), bf16)
    dma = pltpu.SemaphoreType.DMA
    return pl.pallas_call(
        functools.partial(scatter_kernel, planes, chunks),
        out_shape=jax.ShapeDtypeStruct((2, norb * 12, 128), bf16),
        in_specs=[pl.BlockSpec(memory_space=pltpu.VMEM), pl.BlockSpec(memory_space=pltpu.VMEM),
                  pl.BlockSpec(memory_space=pl.ANY)],
        out_specs=pl.BlockSpec(memory_space=pltpu.VMEM),
        scratch_shapes=[
            pltpu.VMEM((n_walkers, own_g), bf16),
            pltpu.VMEM((2, 2, n_walkers // 2, 2 * own_g), bf16),
            pltpu.VMEM((norb, 2 * own_g, 128), bf16),
            slots, slots, slots, slots,
            dma((2,)), dma((chunks,)), dma((chunks,)), dma((chunks,)), dma((chunks,)), dma((chunks,)),
            dma((chunks, planes)), dma((chunks, planes)), dma((chunks, planes)), dma((chunks, planes)),
            dma((chunks,)), dma((chunks,)),
        ],
        compiler_params=pltpu.CompilerParams(
            collective_id=0, has_side_effects=True, vmem_limit_bytes=58 * 2 ** 20),
        cost_estimate=pl.CostEstimate(
            flops=2 * n_walkers * norb * 256 * own_g, bytes_accessed=norb * own_g * 512, transcendentals=0),
    )(shifted, jnp.asarray(row_orders(planes), bf16), chol_t)


def body(planes, walkers, inv_intersection, trial_orbs, cholesky, aux_fields):
    me = lax.axis_index("blk")
    core, z = me % 2, me // 4
    rotated = jnp.einsum(
        "wpi,wij->wpj", walkers, inv_intersection, preferred_element_type=f32
    ).astype(bf16)
    own_half = jnp.einsum("pi,gpq->giq", trial_orbs, cholesky, preferred_element_type=f32).astype(bf16)
    everyone = lax.all_gather(rotated, "blk", axis=0, tiled=True)
    chol_t = jnp.transpose(cholesky, (1, 0, 2))
    force_bias = jnp.einsum("giq,wqi->wg", own_half, everyone, preferred_element_type=f32)
    shifted = (aux_fields + bias_step * force_bias).astype(bf16)
    norb = walkers.shape[1]
    summed = reduced_potential(shifted, chol_t, planes)
    summed = summed.reshape(2, norb // 2, 24, 128)
    straight = summed[:, :, :16].reshape(2, norb, 8, 128)
    mixed = summed[:, :, 16:].reshape(2, norb // 2, 2, 4, 128)
    mixed = jnp.where(z % 2 == 1, mixed[:, :, ::-1], mixed).reshape(2, norb, 4, 128)
    mine = jnp.where(core == 0, straight[:, :, :6],
                     jnp.concatenate([straight[:, :, 6:], mixed], axis=2))
    potential = jnp.transpose((root_step * mine.astype(f32)).astype(bf16), (2, 1, 0, 3))
    potential = potential.reshape(6, norb, norb)
    taylor_term = walkers
    total = walkers.astype(f32)
    for degree in range(1, 5):
        product = jnp.einsum("wpq,wqi->wpi", potential, taylor_term, preferred_element_type=f32)
        taylor_term = (product / degree).astype(bf16)
        total = total + taylor_term.astype(f32)
    new_walkers = total.astype(bf16)
    intersection = jnp.einsum("pi,wpj->wij", trial_orbs, new_walkers, preferred_element_type=f32)
    return (new_walkers, intersection)


def solution(mesh):
    planes = mesh.shape["blk"] // 4
    return jax.shard_map(
        functools.partial(body, planes),
        mesh=mesh,
        in_specs=(
            P(("groups", "blk"), None, None),
            P(("groups", "blk"), None, None),
            P(),
            P(("groups", "blk"), None, None),
            P("groups", "blk"),
        ),
        out_specs=(P(("groups", "blk"), None, None), P(("groups", "blk"), None, None)),
        check_vma=False,
    )
```

```python
import functools

import jax
import jax.numpy as jnp
import numpy as np
from jax import lax
from jax.experimental import pallas as pl
from jax.experimental.pallas import tpu as pltpu
from jax.sharding import PartitionSpec as P

root_step = 0.1
bias_step = 0.5
MESH = pl.DeviceIdType.MESH
bf16 = jnp.bfloat16
f32 = jnp.float32


def row_orders(planes):
    half = planes * 12
    order = np.zeros((2, 2, half), np.int64)
    for parity in range(2):
        for y in range(2):
            for m in range(half):
                if m < planes * 8:
                    dest, within = m // 8, m % 8
                else:
                    rest = m - planes * 8
                    side = (rest % 8) // 4
                    dest = 2 * (rest // 8) + (side if parity == 0 else 1 - side)
                    within = 8 + rest % 4
                order[parity, y, m] = (dest * 2 + y) * 12 + within
    return order.reshape(-1)[:, None] == np.arange(2 * half)[None, :]


def scatter_kernel(planes, chunks, s_ref, perm_ref, chol_ref, out_ref,
                   sib_s, sp, raw, turned, ysend, held, up, down,
                   s_sem, load_sem, chol_send, chol_recv, y_send, y_recv,
                   up_send, up_recv, down_send, down_recv, out_send, out_recv):
    own_g, norb, _ = chol_ref.shape
    span = norb // chunks
    rows = span * 12
    half = planes * 12
    me = lax.axis_index("blk")
    core = lax.rem(me, 2)
    y = lax.rem(lax.div(me, 2), 2)
    z = lax.div(me, 4)
    sibling = me + 1 - 2 * core
    across = me + 2 - 4 * y
    above = me + 4
    below = me - 4
    not_first, not_last = z > 0, z < planes - 1

    barrier = pltpu.get_barrier_semaphore()
    pl.semaphore_signal(barrier, inc=1, device_id={"blk": sibling}, device_id_type=MESH)
    pl.semaphore_signal(barrier, inc=1, device_id={"blk": across}, device_id_type=MESH)

    @pl.when(not_first)
    def _():
        pl.semaphore_signal(barrier, inc=1, device_id={"blk": below}, device_id_type=MESH)

    @pl.when(not_last)
    def _():
        pl.semaphore_signal(barrier, inc=1, device_id={"blk": above}, device_id_type=MESH)

    peers = 2 + jnp.where(not_first, 1, 0) + jnp.where(not_last, 1, 0)
    pl.semaphore_wait(barrier, peers)

    def remote(src, dst, send, recv, target):
        return pltpu.make_async_remote_copy(
            src_ref=src, dst_ref=dst, send_sem=send, recv_sem=recv,
            device_id={"blk": target}, device_id_type=MESH)

    def chol_load(k):
        return pltpu.make_async_copy(
            chol_ref.at[:, pl.ds(pl.multiple_of(k * span, span), span),
                        pl.ds(pl.multiple_of(core * 128, 128), 128)],
            raw.at[pl.ds(0, own_g), pl.ds(pl.multiple_of(k * span, span), span)], load_sem.at[k])

    def chol_swap(k):
        return remote(
            chol_ref.at[:, pl.ds(pl.multiple_of(k * span, span), span),
                        pl.ds(pl.multiple_of((1 - core) * 128, 128), 128)],
            raw.at[pl.ds(own_g, own_g), pl.ds(pl.multiple_of(k * span, span), span)],
            chol_send.at[k], chol_recv.at[k], sibling)

    def y_copy(k):
        return remote(ysend.at[k], held.at[k], y_send.at[k], y_recv.at[k], across)

    def out_copy(k):
        piece = out_ref.at[core, pl.ds(pl.multiple_of(k * rows, 16), rows)]
        return remote(piece, piece, out_send.at[k], out_recv.at[k], sibling)

    s_copy = remote(s_ref, sib_s, s_sem.at[0], s_sem.at[1], sibling)
    s_copy.start()

    def begin(k, carry):
        chol_load(k).start()
        chol_swap(k).start()
        return carry

    lax.fori_loop(0, chunks, begin, 0)
    s_copy.wait()
    for parity in range(2):
        for side in range(2):
            pick = perm_ref[pl.ds((parity * 2 + side) * half, half), :]
            sp[parity, side, :, 0:own_g] = jnp.dot(
                pick, s_ref[...], preferred_element_type=f32).astype(bf16)
            sp[parity, side, :, own_g:] = jnp.dot(
                pick, sib_s[...], preferred_element_type=f32).astype(bf16)

    low = lax.broadcasted_iota(jnp.int32, (8, 128), 0) < 4

    def products(k, side, dst, add):
        def quad(j, carry):
            slot = lax.rem(k, 2)
            r = [jnp.dot(sp[i % 2, side], turned[slot, j * 4 + i], preferred_element_type=f32)
                 for i in range(4)]
            at = pl.ds(pl.multiple_of(j * 48, 48), 48)
            for d in range(planes):
                pieces = []
                mixed = slice(planes * 8 + (d // 2) * 8, planes * 8 + (d // 2) * 8 + 8)
                for i in (0, 2):
                    even, odd = r[i][mixed], r[i + 1][mixed]
                    pieces += [r[i][d * 8:d * 8 + 8], r[i + 1][d * 8:d * 8 + 8],
                               jnp.where(low, even, odd) if d % 2 == 0 else jnp.where(low, odd, even)]
                value = jnp.concatenate(pieces, axis=0)
                if add:
                    value = value + dst[k, d, at].astype(f32)
                dst[k, d, at] = value.astype(bf16)
            return carry

        lax.fori_loop(0, span // 4, quad, 0)

    def hop(k, d, buf, send, recv, has_source, target):
        @pl.when(has_source)
        def _():
            remote(buf.at[k, d], buf.at[k, d], send.at[k, d], recv.at[k, d], target).wait_recv()
            buf[k, d] = (buf[k, d].astype(f32) + held[k, d].astype(f32)).astype(bf16)
            remote(buf.at[k, d], buf.at[k, d], send.at[k, d], recv.at[k, d], target).start()

        @pl.when(jnp.logical_not(has_source))
        def _():
            remote(held.at[k, d], buf.at[k, d], send.at[k, d], recv.at[k, d], target).start()

    def step(t, carry):
        @pl.when(t < chunks)
        def _():
            chol_load(t).wait()
            chol_swap(t).wait_recv()
            columns = pl.ds(pl.multiple_of(t * span, span), span)

            def turn(b, carry):
                at = pl.ds(pl.multiple_of(b * 16, 16), 16)
                turned[lax.rem(t, 2), :, at, :] = jnp.swapaxes(raw[at, columns, :], 0, 1)
                return carry

            lax.fori_loop(0, 2 * own_g // 16, turn, 0)
            products(t, 1 - y, ysend, False)
            y_copy(t).start()

        @pl.when(jnp.logical_and(t >= 1, t <= chunks))
        def _():
            k = t - 1
            y_copy(k).wait_recv()
            products(k, y, held, True)

        ku = t - 1 - z

        @pl.when(jnp.logical_and(ku >= 0, ku < chunks))
        def _():
            for d in range(1, planes):
                @pl.when(d > z)
                def _():
                    hop(ku, d, up, up_send, up_recv, not_first, above)

        kd = t - planes + z

        @pl.when(jnp.logical_and(kd >= 0, kd < chunks))
        def _():
            for d in range(planes - 1):
                @pl.when(d < z)
                def _():
                    hop(kd, d, down, down_send, down_recv, not_last, below)

        kf = t - planes

        @pl.when(jnp.logical_and(kf >= 0, kf < chunks))
        def _():
            at = pl.ds(pl.multiple_of(kf * rows, 16), rows)

            @pl.when(jnp.logical_not(not_first))
            def _():
                remote(down.at[kf, z], down.at[kf, z], down_send.at[kf, z], down_recv.at[kf, z], above).wait_recv()
                out_ref[core, at] = (held[kf, z].astype(f32) + down[kf, z].astype(f32)).astype(bf16)

            @pl.when(jnp.logical_not(not_last))
            def _():
                remote(up.at[kf, z], up.at[kf, z], up_send.at[kf, z], up_recv.at[kf, z], below).wait_recv()
                out_ref[core, at] = (held[kf, z].astype(f32) + up[kf, z].astype(f32)).astype(bf16)

            @pl.when(jnp.logical_and(not_first, not_last))
            def _():
                remote(down.at[kf, z], down.at[kf, z], down_send.at[kf, z], down_recv.at[kf, z], above).wait_recv()
                remote(up.at[kf, z], up.at[kf, z], up_send.at[kf, z], up_recv.at[kf, z], below).wait_recv()
                out_ref[core, at] = (
                    held[kf, z].astype(f32) + up[kf, z].astype(f32) + down[kf, z].astype(f32)
                ).astype(bf16)

            out_copy(kf).start()

        return carry

    lax.fori_loop(0, chunks + planes, step, 0)

    def finish(k, carry):
        chol_swap(k).wait_send()
        y_copy(k).wait_send()
        for d in range(planes):
            @pl.when(d > z)
            def _():
                remote(up.at[k, d], up.at[k, d], up_send.at[k, d], up_recv.at[k, d], above).wait_send()

            @pl.when(d < z)
            def _():
                remote(down.at[k, d], down.at[k, d], down_send.at[k, d], down_recv.at[k, d], below).wait_send()

        out_copy(k).wait_send()
        other = out_ref.at[1 - core, pl.ds(pl.multiple_of(k * rows, 16), rows)]
        remote(other, other, out_send.at[k], out_recv.at[k], sibling).wait_recv()
        return carry

    lax.fori_loop(0, chunks, finish, 0)


def reduced_potential(shifted, cholesky, planes, chunks=16):
    n_walkers, own_g = shifted.shape
    norb = cholesky.shape[1]
    rows = norb // chunks * 12
    slots = pltpu.VMEM((chunks, planes, rows, 128), bf16)
    dma = pltpu.SemaphoreType.DMA
    return pl.pallas_call(
        functools.partial(scatter_kernel, planes, chunks),
        out_shape=jax.ShapeDtypeStruct((2, norb * 12, 128), bf16),
        in_specs=[pl.BlockSpec(memory_space=pltpu.VMEM), pl.BlockSpec(memory_space=pltpu.VMEM),
                  pl.BlockSpec(memory_space=pl.ANY)],
        out_specs=pl.BlockSpec(memory_space=pltpu.VMEM),
        scratch_shapes=[
            pltpu.VMEM((n_walkers, own_g), bf16),
            pltpu.VMEM((2, 2, n_walkers // 2, 2 * own_g), bf16),
            pltpu.VMEM((2 * own_g, norb, 128), bf16),
            pltpu.VMEM((2, norb // chunks, 2 * own_g, 128), bf16),
            slots, slots, slots, slots,
            dma((2,)), dma((chunks,)), dma((chunks,)), dma((chunks,)), dma((chunks,)), dma((chunks,)),
            dma((chunks, planes)), dma((chunks, planes)), dma((chunks, planes)), dma((chunks, planes)),
            dma((chunks,)), dma((chunks,)),
        ],
        compiler_params=pltpu.CompilerParams(
            collective_id=0, has_side_effects=True, vmem_limit_bytes=58 * 2 ** 20),
        cost_estimate=pl.CostEstimate(
            flops=2 * n_walkers * norb * 256 * own_g, bytes_accessed=norb * own_g * 512, transcendentals=0),
    )(shifted, jnp.asarray(row_orders(planes), bf16), cholesky)


def body(planes, walkers, inv_intersection, trial_orbs, cholesky, aux_fields):
    me = lax.axis_index("blk")
    core, z = lax.rem(me, 2), lax.div(me, 4)
    rotated = jnp.einsum(
        "wpi,wij->wpj", walkers, inv_intersection, preferred_element_type=f32
    ).astype(bf16)
    own_half = jnp.einsum("pi,gpq->giq", trial_orbs, cholesky, preferred_element_type=f32).astype(bf16)
    n_dev = planes * 4
    same_core = lax.all_gather(
        rotated, "blk", axis=0, tiled=True,
        axis_index_groups=[list(range(0, n_dev, 2)), list(range(1, n_dev, 2))])
    same_core, own_half = lax.optimization_barrier((same_core, own_half))
    other_core = lax.ppermute(same_core, "blk", [(i, i ^ 1) for i in range(n_dev)])
    biases = [jnp.einsum("giq,wqi->wg", own_half, some, preferred_element_type=f32)
              for some in (same_core, other_core)]
    biases = [b.reshape(n_dev // 2, 1, -1, b.shape[1]) for b in biases]
    force_bias = jnp.where(core == 0, jnp.concatenate(biases, axis=1),
                           jnp.concatenate(biases[::-1], axis=1)).reshape(aux_fields.shape)
    shifted = (aux_fields + bias_step * force_bias).astype(bf16)
    norb = walkers.shape[1]
    summed = reduced_potential(shifted, cholesky, planes)
    summed = summed.reshape(2, norb // 2, 24, 128)
    straight = summed[:, :, :16].reshape(2, norb, 8, 128)
    mixed = summed[:, :, 16:].reshape(2, norb // 2, 2, 4, 128)
    mixed = jnp.where(lax.rem(z, 2) == 1, mixed[:, :, ::-1], mixed).reshape(2, norb, 4, 128)
    mine = jnp.where(core == 0, straight[:, :, :6],
                     jnp.concatenate([straight[:, :, 6:], mixed], axis=2))
    potential = jnp.transpose((root_step * mine.astype(f32)).astype(bf16), (2, 1, 0, 3))
    potential = potential.reshape(6, norb, norb)
    taylor_term = walkers
    total = walkers.astype(f32)
    for degree in range(1, 5):
        product = jnp.einsum("wpq,wqi->wpi", potential, taylor_term, preferred_element_type=f32)
        taylor_term = (product / degree).astype(bf16)
        total = total + taylor_term.astype(f32)
    new_walkers = total.astype(bf16)
    intersection = jnp.einsum("pi,wpj->wij", trial_orbs, new_walkers, preferred_element_type=f32)
    return (new_walkers, intersection)


def solution(mesh):
    planes = mesh.shape["blk"] // 4
    return jax.shard_map(
        functools.partial(body, planes),
        mesh=mesh,
        in_specs=(
            P(("groups", "blk"), None, None),
            P(("groups", "blk"), None, None),
            P(),
            P(("groups", "blk"), None, None),
            P("groups", "blk"),
        ),
        out_specs=(P(("groups", "blk"), None, None), P(("groups", "blk"), None, None)),
        check_vma=False,
    )
```

```python
import functools

import jax
import jax.numpy as jnp
import numpy as np
from jax import lax
from jax.experimental import pallas as pl
from jax.experimental.pallas import tpu as pltpu
from jax.sharding import PartitionSpec as P

root_step = 0.1
bias_step = 0.5
MESH = pl.DeviceIdType.MESH
bf16 = jnp.bfloat16
f32 = jnp.float32


def row_orders(planes):
    half = planes * 12
    order = np.zeros((2, 2, half), np.int64)
    for parity in range(2):
        for y in range(2):
            for m in range(half):
                if m < planes * 8:
                    dest, within = m // 8, m % 8
                else:
                    rest = m - planes * 8
                    side = (rest % 8) // 4
                    dest = 2 * (rest // 8) + (side if parity == 0 else 1 - side)
                    within = 8 + rest % 4
                order[parity, y, m] = (dest * 2 + y) * 12 + within
    return order.reshape(-1)[:, None] == np.arange(2 * half)[None, :]


def scatter_kernel(planes, chunks, s_ref, perm_ref, chol_ref, out_ref,
                   sib_s, sp, raw, turned, ysend, held, up, down,
                   s_sem, load_sem, chol_send, chol_recv, y_send, y_recv,
                   up_send, up_recv, down_send, down_recv, out_send, out_recv):
    own_g, norb, _ = chol_ref.shape
    span = norb // chunks
    rows = span * 12
    half = planes * 12
    me = lax.axis_index("blk")
    core = lax.rem(me, 2)
    y = lax.rem(lax.div(me, 2), 2)
    z = lax.div(me, 4)
    sibling = me + 1 - 2 * core
    across = me + 2 - 4 * y
    above = me + 4
    below = me - 4
    not_first, not_last = z > 0, z < planes - 1

    barrier = pltpu.get_barrier_semaphore()
    pl.semaphore_signal(barrier, inc=1, device_id={"blk": sibling}, device_id_type=MESH)
    pl.semaphore_signal(barrier, inc=1, device_id={"blk": across}, device_id_type=MESH)

    @pl.when(not_first)
    def _():
        pl.semaphore_signal(barrier, inc=1, device_id={"blk": below}, device_id_type=MESH)

    @pl.when(not_last)
    def _():
        pl.semaphore_signal(barrier, inc=1, device_id={"blk": above}, device_id_type=MESH)

    peers = 2 + jnp.where(not_first, 1, 0) + jnp.where(not_last, 1, 0)
    pl.semaphore_wait(barrier, peers)

    def remote(src, dst, send, recv, target):
        return pltpu.make_async_remote_copy(
            src_ref=src, dst_ref=dst, send_sem=send, recv_sem=recv,
            device_id={"blk": target}, device_id_type=MESH)

    def chol_load(k):
        return pltpu.make_async_copy(
            chol_ref.at[:, pl.ds(pl.multiple_of(k * span, span), span),
                        pl.ds(pl.multiple_of(core * 128, 128), 128)],
            raw.at[pl.ds(0, own_g), pl.ds(pl.multiple_of(k * span, span), span)], load_sem.at[k])

    def chol_swap(k):
        return remote(
            chol_ref.at[:, pl.ds(pl.multiple_of(k * span, span), span),
                        pl.ds(pl.multiple_of((1 - core) * 128, 128), 128)],
            raw.at[pl.ds(own_g, own_g), pl.ds(pl.multiple_of(k * span, span), span)],
            chol_send.at[k], chol_recv.at[k], sibling)

    def y_copy(k):
        return remote(ysend.at[k], held.at[k], y_send.at[k], y_recv.at[k], across)

    def out_copy(k):
        piece = out_ref.at[core, pl.ds(pl.multiple_of(k * rows, 16), rows)]
        return remote(piece, piece, out_send.at[k], out_recv.at[k], sibling)

    s_copy = remote(s_ref, sib_s, s_sem.at[0], s_sem.at[1], sibling)
    s_copy.start()

    def begin(k, carry):
        chol_load(k).start()
        chol_swap(k).start()
        return carry

    lax.fori_loop(0, chunks, begin, 0)
    s_copy.wait()
    for parity in range(2):
        for side in range(2):
            pick = perm_ref[pl.ds((parity * 2 + side) * half, half), :]
            sp[parity, side, :, 0:own_g] = jnp.dot(
                pick, s_ref[...], preferred_element_type=f32).astype(bf16)
            sp[parity, side, :, own_g:] = jnp.dot(
                pick, sib_s[...], preferred_element_type=f32).astype(bf16)

    low = lax.broadcasted_iota(jnp.int32, (8, 128), 0) < 4

    def products(k, side, dst, add):
        def quad(j, carry):
            slot = lax.rem(k, 2)
            r = [jnp.dot(sp[i % 2, side], turned[slot, j * 4 + i], preferred_element_type=f32)
                 for i in range(4)]
            at = pl.ds(pl.multiple_of(j * 48, 48), 48)
            for d in range(planes):
                pieces = []
                mixed = slice(planes * 8 + (d // 2) * 8, planes * 8 + (d // 2) * 8 + 8)
                for i in (0, 2):
                    even, odd = r[i][mixed], r[i + 1][mixed]
                    pieces += [r[i][d * 8:d * 8 + 8], r[i + 1][d * 8:d * 8 + 8],
                               jnp.where(low, even, odd) if d % 2 == 0 else jnp.where(low, odd, even)]
                value = jnp.concatenate(pieces, axis=0)
                if add:
                    value = value + dst[k, d, at].astype(f32)
                dst[k, d, at] = value.astype(bf16)
            return carry

        lax.fori_loop(0, span // 4, quad, 0)

    def hop(k, d, buf, send, recv, has_source, target):
        @pl.when(has_source)
        def _():
            remote(buf.at[k, d], buf.at[k, d], send.at[k, d], recv.at[k, d], target).wait_recv()
            buf[k, d] = (buf[k, d].astype(f32) + held[k, d].astype(f32)).astype(bf16)
            remote(buf.at[k, d], buf.at[k, d], send.at[k, d], recv.at[k, d], target).start()

        @pl.when(jnp.logical_not(has_source))
        def _():
            remote(held.at[k, d], buf.at[k, d], send.at[k, d], recv.at[k, d], target).start()

    def step(t, carry):
        @pl.when(t < chunks)
        def _():
            chol_load(t).wait()
            chol_swap(t).wait_recv()
            columns = pl.ds(pl.multiple_of(t * span, span), span)

            def turn(b, carry):
                at = pl.ds(pl.multiple_of(b * 16, 16), 16)
                turned[lax.rem(t, 2), :, at, :] = jnp.swapaxes(raw[at, columns, :], 0, 1)
                return carry

            lax.fori_loop(0, 2 * own_g // 16, turn, 0)
            products(t, 1 - y, ysend, False)
            y_copy(t).start()

        @pl.when(jnp.logical_and(t >= 1, t <= chunks))
        def _():
            k = t - 1
            y_copy(k).wait_recv()
            products(k, y, held, True)

        ku = t - 1 - z

        @pl.when(jnp.logical_and(ku >= 0, ku < chunks))
        def _():
            for d in range(1, planes):
                @pl.when(d > z)
                def _():
                    hop(ku, d, up, up_send, up_recv, not_first, above)

        kd = t - planes + z

        @pl.when(jnp.logical_and(kd >= 0, kd < chunks))
        def _():
            for d in range(planes - 1):
                @pl.when(d < z)
                def _():
                    hop(kd, d, down, down_send, down_recv, not_last, below)

        kf = t - planes

        @pl.when(jnp.logical_and(kf >= 0, kf < chunks))
        def _():
            at = pl.ds(pl.multiple_of(kf * rows, 16), rows)

            @pl.when(jnp.logical_not(not_first))
            def _():
                remote(down.at[kf, z], down.at[kf, z], down_send.at[kf, z], down_recv.at[kf, z], above).wait_recv()
                out_ref[core, at] = (held[kf, z].astype(f32) + down[kf, z].astype(f32)).astype(bf16)

            @pl.when(jnp.logical_not(not_last))
            def _():
                remote(up.at[kf, z], up.at[kf, z], up_send.at[kf, z], up_recv.at[kf, z], below).wait_recv()
                out_ref[core, at] = (held[kf, z].astype(f32) + up[kf, z].astype(f32)).astype(bf16)

            @pl.when(jnp.logical_and(not_first, not_last))
            def _():
                remote(down.at[kf, z], down.at[kf, z], down_send.at[kf, z], down_recv.at[kf, z], above).wait_recv()
                remote(up.at[kf, z], up.at[kf, z], up_send.at[kf, z], up_recv.at[kf, z], below).wait_recv()
                out_ref[core, at] = (
                    held[kf, z].astype(f32) + up[kf, z].astype(f32) + down[kf, z].astype(f32)
                ).astype(bf16)

            out_copy(kf).start()

        return carry

    lax.fori_loop(0, chunks + planes, step, 0)

    def finish(k, carry):
        chol_swap(k).wait_send()
        y_copy(k).wait_send()
        for d in range(planes):
            @pl.when(d > z)
            def _():
                remote(up.at[k, d], up.at[k, d], up_send.at[k, d], up_recv.at[k, d], above).wait_send()

            @pl.when(d < z)
            def _():
                remote(down.at[k, d], down.at[k, d], down_send.at[k, d], down_recv.at[k, d], below).wait_send()

        out_copy(k).wait_send()
        other = out_ref.at[1 - core, pl.ds(pl.multiple_of(k * rows, 16), rows)]
        remote(other, other, out_send.at[k], out_recv.at[k], sibling).wait_recv()
        return carry

    lax.fori_loop(0, chunks, finish, 0)


def reduced_potential(shifted, cholesky, planes, chunks=16):
    n_walkers, own_g = shifted.shape
    norb = cholesky.shape[1]
    rows = norb // chunks * 12
    slots = pltpu.VMEM((chunks, planes, rows, 128), bf16)
    dma = pltpu.SemaphoreType.DMA
    return pl.pallas_call(
        functools.partial(scatter_kernel, planes, chunks),
        out_shape=jax.ShapeDtypeStruct((2, norb * 12, 128), bf16),
        in_specs=[pl.BlockSpec(memory_space=pltpu.VMEM), pl.BlockSpec(memory_space=pltpu.VMEM),
                  pl.BlockSpec(memory_space=pl.ANY)],
        out_specs=pl.BlockSpec(memory_space=pltpu.VMEM),
        scratch_shapes=[
            pltpu.VMEM((n_walkers, own_g), bf16),
            pltpu.VMEM((2, 2, n_walkers // 2, 2 * own_g), bf16),
            pltpu.VMEM((2 * own_g, norb, 128), bf16),
            pltpu.VMEM((2, norb // chunks, 2 * own_g, 128), bf16),
            slots, slots, slots, slots,
            dma((2,)), dma((chunks,)), dma((chunks,)), dma((chunks,)), dma((chunks,)), dma((chunks,)),
            dma((chunks, planes)), dma((chunks, planes)), dma((chunks, planes)), dma((chunks, planes)),
            dma((chunks,)), dma((chunks,)),
        ],
        compiler_params=pltpu.CompilerParams(
            collective_id=0, has_side_effects=True, vmem_limit_bytes=58 * 2 ** 20),
        cost_estimate=pl.CostEstimate(
            flops=2 * n_walkers * norb * 256 * own_g, bytes_accessed=norb * own_g * 512, transcendentals=0),
    )(shifted, jnp.asarray(row_orders(planes), bf16), cholesky)


def bias_kernel(planes, rot_ref, trial_ref, chol_ref, aux_ref, out_ref,
                chol, part, half_rot, gathered, turned,
                load_sem, own_sem, z_recv, up_send, down_send, y_send, y_recv, sib_send, sib_recv):
    own_g, norb, _ = chol_ref.shape
    count, nocc, _ = rot_ref.shape
    n_walkers = gathered.shape[0]
    blocks = own_g // 16
    me = lax.axis_index("blk")
    core = lax.rem(me, 2)
    y = lax.rem(lax.div(me, 2), 2)
    z = lax.div(me, 4)
    sibling = me + 1 - 2 * core
    across = me + 2 - 4 * y
    above = me + 4
    below = me - 4
    not_first, not_last = z > 0, z < planes - 1

    def load(b):
        at = pl.ds(b * 16, 16)
        return pltpu.make_async_copy(chol_ref.at[at], chol.at[at], load_sem.at[b])

    for b in range(blocks):
        load(b).start()

    barrier = pltpu.get_barrier_semaphore()
    pl.semaphore_signal(barrier, inc=1, device_id={"blk": sibling}, device_id_type=MESH)
    pl.semaphore_signal(barrier, inc=1, device_id={"blk": across}, device_id_type=MESH)

    @pl.when(not_first)
    def _():
        pl.semaphore_signal(barrier, inc=1, device_id={"blk": below}, device_id_type=MESH)

    @pl.when(not_last)
    def _():
        pl.semaphore_signal(barrier, inc=1, device_id={"blk": above}, device_id_type=MESH)

    peers = 2 + jnp.where(not_first, 1, 0) + jnp.where(not_last, 1, 0)
    pl.semaphore_wait(barrier, peers)

    def move(plane, column, owner_core, send, recv, target):
        piece = gathered.at[pl.ds(((plane * 2 + column) * 2 + owner_core) * count, count)]
        return pltpu.make_async_remote_copy(
            src_ref=piece, dst_ref=piece, send_sem=send, recv_sem=recv,
            device_id={"blk": target}, device_id_type=MESH)

    def go_up(plane):
        return move(plane, y, core, up_send.at[plane], z_recv.at[plane], above)

    def go_down(plane):
        return move(plane, y, core, down_send.at[plane], z_recv.at[plane], below)

    def go_across(plane):
        return move(plane, y, core, y_send.at[plane], y_recv.at[plane], across)

    def from_across(plane):
        return move(plane, 1 - y, core, y_send.at[plane], y_recv.at[plane], across)

    def go_sibling(plane, column):
        return move(plane, column, core, sib_send.at[plane, column], sib_recv.at[plane, column], sibling)

    def from_sibling(plane, column):
        return move(plane, column, 1 - core, sib_send.at[plane, column], sib_recv.at[plane, column], sibling)

    own = pltpu.make_async_copy(rot_ref, gathered.at[pl.ds(me * count, count)], own_sem)
    own.start()
    own.wait()

    @pl.when(not_last)
    def _():
        go_up(z).start()

    @pl.when(not_first)
    def _():
        go_down(z).start()

    go_across(z).start()
    go_sibling(z, y).start()

    def make_half(b):
        load(b).wait()

        def one(j, carry):
            part[j] = jnp.dot(trial_ref[...], chol[b * 16 + j], preferred_element_type=f32).astype(bf16)
            return carry

        lax.fori_loop(0, 16, one, 0)

        def turn(i, carry):
            at = pl.ds(pl.multiple_of(i * 16, 16), 16)
            half_rot[at, pl.ds(b * 16, 16), :] = jnp.swapaxes(part[:, at, :], 0, 1)
            return carry

        lax.fori_loop(0, nocc // 16, turn, 0)

    done = 0
    for t in range(1, planes + 1):
        until = -(-blocks * t // planes)
        for b in range(done, until):
            make_half(b)
        done = until
        if t < planes:
            low, high = z - t, z + t

            @pl.when(low >= 0)
            def _():
                go_up(low).wait_recv()

                @pl.when(not_last)
                def _():
                    go_up(low).start()

                go_across(low).start()
                go_sibling(low, y).start()

            @pl.when(high < planes)
            def _():
                go_down(high).wait_recv()

                @pl.when(not_first)
                def _():
                    go_down(high).start()

                go_across(high).start()
                go_sibling(high, y).start()

        def pass_on(plane):
            from_across(plane).wait_recv()
            go_sibling(plane, 1 - y).start()

        if t == 1:
            pass_on(z)
        else:
            @pl.when(z - (t - 1) >= 0)
            def _():
                pass_on(z - (t - 1))

            @pl.when(z + (t - 1) < planes)
            def _():
                pass_on(z + (t - 1))

    for plane in range(planes):
        for column in range(2):
            from_sibling(plane, column).wait_recv()

    def turn_walkers(w, carry):
        rows = pl.ds(pl.multiple_of(w * 16, 16), 16)

        def turn(i, carry):
            at = pl.ds(pl.multiple_of(i * 16, 16), 16)
            turned[at, rows, :] = jnp.swapaxes(gathered[rows, at, :], 0, 1)
            return carry

        return lax.fori_loop(0, nocc // 16, turn, carry)

    lax.fori_loop(0, n_walkers // 16, turn_walkers, 0)

    def contract(i, total):
        for j in range(4):
            total = total + lax.dot_general(
                turned[i * 4 + j], half_rot[i * 4 + j], (((1,), (1,)), ((), ())),
                preferred_element_type=f32)
        return total

    bias = lax.fori_loop(0, nocc // 4, contract, jnp.zeros((n_walkers, own_g), f32))
    out_ref[...] = (aux_ref[...] + bias_step * bias).astype(bf16)

    for plane in range(planes):
        @pl.when(jnp.logical_and(plane <= z, not_last))
        def _():
            go_up(plane).wait_send()

        @pl.when(jnp.logical_and(plane >= z, not_first))
        def _():
            go_down(plane).wait_send()

        go_across(plane).wait_send()
        for column in range(2):
            go_sibling(plane, column).wait_send()


def shifted_fields(rotated, trial_t, cholesky, aux_fields, planes):
    own_g, norb, _ = cholesky.shape
    nocc = trial_t.shape[0]
    n_walkers = aux_fields.shape[0]
    vmem = pl.BlockSpec(memory_space=pltpu.VMEM)
    dma = pltpu.SemaphoreType.DMA
    return pl.pallas_call(
        functools.partial(bias_kernel, planes),
        out_shape=jax.ShapeDtypeStruct((n_walkers, own_g), bf16),
        in_specs=[vmem, vmem, pl.BlockSpec(memory_space=pl.ANY), vmem],
        out_specs=vmem,
        scratch_shapes=[
            pltpu.VMEM((own_g, norb, norb), bf16),
            pltpu.VMEM((16, nocc, norb), bf16),
            pltpu.VMEM((nocc, own_g, norb), bf16),
            pltpu.VMEM((n_walkers, nocc, norb), bf16),
            pltpu.VMEM((nocc, n_walkers, norb), bf16),
            dma((own_g // 16,)), dma(()), dma((planes,)), dma((planes,)), dma((planes,)),
            dma((planes,)), dma((planes,)), dma((planes, 2)), dma((planes, 2)),
        ],
        compiler_params=pltpu.CompilerParams(
            collective_id=1, has_side_effects=True, vmem_limit_bytes=58 * 2 ** 20),
        cost_estimate=pl.CostEstimate(
            flops=2 * own_g * nocc * norb * (norb + n_walkers),
            bytes_accessed=own_g * norb * norb * 2, transcendentals=0),
    )(rotated, trial_t, cholesky, aux_fields)


def body(planes, walkers, inv_intersection, trial_orbs, cholesky, aux_fields):
    me = lax.axis_index("blk")
    core, z = lax.rem(me, 2), lax.div(me, 4)
    rotated = jnp.einsum(
        "wpi,wij->wjp", walkers, inv_intersection, preferred_element_type=f32
    ).astype(bf16)
    shifted = shifted_fields(rotated, trial_orbs.T, cholesky, aux_fields, planes)
    norb = walkers.shape[1]
    summed = reduced_potential(shifted, cholesky, planes)
    summed = summed.reshape(2, norb // 2, 24, 128)
    straight = summed[:, :, :16].reshape(2, norb, 8, 128)
    mixed = summed[:, :, 16:].reshape(2, norb // 2, 2, 4, 128)
    mixed = jnp.where(lax.rem(z, 2) == 1, mixed[:, :, ::-1], mixed).reshape(2, norb, 4, 128)
    mine = jnp.where(core == 0, straight[:, :, :6],
                     jnp.concatenate([straight[:, :, 6:], mixed], axis=2))
    potential = jnp.transpose((root_step * mine.astype(f32)).astype(bf16), (2, 1, 0, 3))
    potential = potential.reshape(6, norb, norb)
    taylor_term = walkers
    total = walkers.astype(f32)
    for degree in range(1, 5):
        product = jnp.einsum("wpq,wqi->wpi", potential, taylor_term, preferred_element_type=f32)
        taylor_term = (product / degree).astype(bf16)
        total = total + taylor_term.astype(f32)
    new_walkers = total.astype(bf16)
    intersection = jnp.einsum("pi,wpj->wij", trial_orbs, new_walkers, preferred_element_type=f32)
    return (new_walkers, intersection)


def solution(mesh):
    planes = mesh.shape["blk"] // 4
    return jax.shard_map(
        functools.partial(body, planes),
        mesh=mesh,
        in_specs=(
            P(("groups", "blk"), None, None),
            P(("groups", "blk"), None, None),
            P(),
            P(("groups", "blk"), None, None),
            P("groups", "blk"),
        ),
        out_specs=(P(("groups", "blk"), None, None), P(("groups", "blk"), None, None)),
        check_vma=False,
    )
```

```python
import functools

import jax
import jax.numpy as jnp
import numpy as np
from jax import lax
from jax.experimental import pallas as pl
from jax.experimental.pallas import tpu as pltpu
from jax.sharding import PartitionSpec as P

root_step = 0.1
bias_step = 0.5
MESH = pl.DeviceIdType.MESH
bf16 = jnp.bfloat16
f32 = jnp.float32


def row_orders(planes):
    half = planes * 12
    order = np.zeros((2, 2, half), np.int64)
    for parity in range(2):
        for y in range(2):
            for m in range(half):
                if m < planes * 8:
                    dest, within = m // 8, m % 8
                else:
                    rest = m - planes * 8
                    side = (rest % 8) // 4
                    dest = 2 * (rest // 8) + (side if parity == 0 else 1 - side)
                    within = 8 + rest % 4
                order[parity, y, m] = (dest * 2 + y) * 12 + within
    return order.reshape(-1)[:, None] == np.arange(2 * half)[None, :]


def scatter_kernel(planes, chunks, ahead, s_ref, perm_ref, chol_ref, out_ref,
                   sib_s, sp, raw, turned, ysend, held, up, down,
                   s_sem, load_sem, chol_send, chol_recv, y_send, y_recv,
                   up_send, up_recv, down_send, down_recv, out_send, out_recv):
    own_g, norb, _ = chol_ref.shape
    span = norb // chunks
    rows = span * 12
    half = planes * 12
    me = lax.axis_index("blk")
    core = lax.rem(me, 2)
    y = lax.rem(lax.div(me, 2), 2)
    z = lax.div(me, 4)
    sibling = me + 1 - 2 * core
    across = me + 2 - 4 * y
    above = me + 4
    below = me - 4
    not_first, not_last = z > 0, z < planes - 1

    barrier = pltpu.get_barrier_semaphore()
    pl.semaphore_signal(barrier, inc=1, device_id={"blk": sibling}, device_id_type=MESH)
    pl.semaphore_signal(barrier, inc=1, device_id={"blk": across}, device_id_type=MESH)

    @pl.when(not_first)
    def _():
        pl.semaphore_signal(barrier, inc=1, device_id={"blk": below}, device_id_type=MESH)

    @pl.when(not_last)
    def _():
        pl.semaphore_signal(barrier, inc=1, device_id={"blk": above}, device_id_type=MESH)

    peers = 2 + jnp.where(not_first, 1, 0) + jnp.where(not_last, 1, 0)
    pl.semaphore_wait(barrier, peers)

    def remote(src, dst, send, recv, target):
        return pltpu.make_async_remote_copy(
            src_ref=src, dst_ref=dst, send_sem=send, recv_sem=recv,
            device_id={"blk": target}, device_id_type=MESH)

    def chol_load(k):
        return pltpu.make_async_copy(
            chol_ref.at[:, pl.ds(pl.multiple_of(k * span, span), span),
                        pl.ds(pl.multiple_of(core * 128, 128), 128)],
            raw.at[pl.ds(0, own_g), pl.ds(pl.multiple_of(k * span, span), span)], load_sem.at[k])

    def chol_swap(k):
        return remote(
            chol_ref.at[:, pl.ds(pl.multiple_of(k * span, span), span),
                        pl.ds(pl.multiple_of((1 - core) * 128, 128), 128)],
            raw.at[pl.ds(own_g, own_g), pl.ds(pl.multiple_of(k * span, span), span)],
            chol_send.at[k], chol_recv.at[k], sibling)

    def y_copy(k):
        return remote(ysend.at[k], held.at[k], y_send.at[k], y_recv.at[k], across)

    def out_copy(k):
        piece = out_ref.at[core, pl.ds(pl.multiple_of(k * rows, 16), rows)]
        return remote(piece, piece, out_send.at[k], out_recv.at[k], sibling)

    s_copy = remote(s_ref, sib_s, s_sem.at[0], s_sem.at[1], sibling)
    s_copy.start()

    def begin(k, carry):
        chol_load(k).start()
        chol_swap(k).start()
        return carry

    lax.fori_loop(0, ahead, begin, 0)
    s_copy.wait()
    for parity in range(2):
        for side in range(2):
            pick = perm_ref[pl.ds((parity * 2 + side) * half, half), :]
            sp[parity, side, :, 0:own_g] = jnp.dot(
                pick, s_ref[...], preferred_element_type=f32).astype(bf16)
            sp[parity, side, :, own_g:] = jnp.dot(
                pick, sib_s[...], preferred_element_type=f32).astype(bf16)

    low = lax.broadcasted_iota(jnp.int32, (8, 128), 0) < 4

    def products(k, side, dst, add):
        def quad(j, carry):
            slot = lax.rem(k, 2)
            r = [jnp.dot(sp[i % 2, side], turned[slot, j * 4 + i], preferred_element_type=f32)
                 for i in range(4)]
            at = pl.ds(pl.multiple_of(j * 48, 48), 48)
            for d in range(planes):
                pieces = []
                mixed = slice(planes * 8 + (d // 2) * 8, planes * 8 + (d // 2) * 8 + 8)
                for i in (0, 2):
                    even, odd = r[i][mixed], r[i + 1][mixed]
                    pieces += [r[i][d * 8:d * 8 + 8], r[i + 1][d * 8:d * 8 + 8],
                               jnp.where(low, even, odd) if d % 2 == 0 else jnp.where(low, odd, even)]
                value = jnp.concatenate(pieces, axis=0)
                if add:
                    value = value + dst[k, d, at].astype(f32)
                dst[k, d, at] = value.astype(bf16)
            return carry

        lax.fori_loop(0, span // 4, quad, 0)

    def hop(k, d, buf, send, recv, has_source, target):
        @pl.when(has_source)
        def _():
            remote(buf.at[k, d], buf.at[k, d], send.at[k, d], recv.at[k, d], target).wait_recv()
            buf[k, d] = (buf[k, d].astype(f32) + held[k, d].astype(f32)).astype(bf16)
            remote(buf.at[k, d], buf.at[k, d], send.at[k, d], recv.at[k, d], target).start()

        @pl.when(jnp.logical_not(has_source))
        def _():
            remote(held.at[k, d], buf.at[k, d], send.at[k, d], recv.at[k, d], target).start()

    def step(t, carry):
        @pl.when(t + ahead < chunks)
        def _():
            begin(t + ahead, 0)

        @pl.when(t < chunks)
        def _():
            chol_load(t).wait()
            chol_swap(t).wait_recv()
            columns = pl.ds(pl.multiple_of(t * span, span), span)

            def turn(b, carry):
                at = pl.ds(pl.multiple_of(b * 16, 16), 16)
                turned[lax.rem(t, 2), :, at, :] = jnp.swapaxes(raw[at, columns, :], 0, 1)
                return carry

            lax.fori_loop(0, 2 * own_g // 16, turn, 0)
            products(t, 1 - y, ysend, False)
            y_copy(t).start()

        @pl.when(jnp.logical_and(t >= 1, t <= chunks))
        def _():
            k = t - 1
            y_copy(k).wait_recv()
            products(k, y, held, True)

        ku = t - 1 - z

        @pl.when(jnp.logical_and(ku >= 0, ku < chunks))
        def _():
            for d in range(1, planes):
                @pl.when(d > z)
                def _():
                    hop(ku, d, up, up_send, up_recv, not_first, above)

        kd = t - planes + z

        @pl.when(jnp.logical_and(kd >= 0, kd < chunks))
        def _():
            for d in range(planes - 1):
                @pl.when(d < z)
                def _():
                    hop(kd, d, down, down_send, down_recv, not_last, below)

        kf = t - planes

        @pl.when(jnp.logical_and(kf >= 0, kf < chunks))
        def _():
            at = pl.ds(pl.multiple_of(kf * rows, 16), rows)

            @pl.when(jnp.logical_not(not_first))
            def _():
                remote(down.at[kf, z], down.at[kf, z], down_send.at[kf, z], down_recv.at[kf, z], above).wait_recv()
                out_ref[core, at] = (held[kf, z].astype(f32) + down[kf, z].astype(f32)).astype(bf16)

            @pl.when(jnp.logical_not(not_last))
            def _():
                remote(up.at[kf, z], up.at[kf, z], up_send.at[kf, z], up_recv.at[kf, z], below).wait_recv()
                out_ref[core, at] = (held[kf, z].astype(f32) + up[kf, z].astype(f32)).astype(bf16)

            @pl.when(jnp.logical_and(not_first, not_last))
            def _():
                remote(down.at[kf, z], down.at[kf, z], down_send.at[kf, z], down_recv.at[kf, z], above).wait_recv()
                remote(up.at[kf, z], up.at[kf, z], up_send.at[kf, z], up_recv.at[kf, z], below).wait_recv()
                out_ref[core, at] = (
                    held[kf, z].astype(f32) + up[kf, z].astype(f32) + down[kf, z].astype(f32)
                ).astype(bf16)

            out_copy(kf).start()

        return carry

    lax.fori_loop(0, chunks + planes, step, 0)

    def finish(k, carry):
        chol_swap(k).wait_send()
        y_copy(k).wait_send()
        for d in range(planes):
            @pl.when(d > z)
            def _():
                remote(up.at[k, d], up.at[k, d], up_send.at[k, d], up_recv.at[k, d], above).wait_send()

            @pl.when(d < z)
            def _():
                remote(down.at[k, d], down.at[k, d], down_send.at[k, d], down_recv.at[k, d], below).wait_send()

        out_copy(k).wait_send()
        other = out_ref.at[1 - core, pl.ds(pl.multiple_of(k * rows, 16), rows)]
        remote(other, other, out_send.at[k], out_recv.at[k], sibling).wait_recv()
        return carry

    lax.fori_loop(0, chunks, finish, 0)


def reduced_potential(shifted, cholesky, planes, chunks=16):
    n_walkers, own_g = shifted.shape
    norb = cholesky.shape[1]
    rows = norb // chunks * 12
    slots = pltpu.VMEM((chunks, planes, rows, 128), bf16)
    dma = pltpu.SemaphoreType.DMA
    return pl.pallas_call(
        functools.partial(scatter_kernel, planes, chunks, 3),
        out_shape=jax.ShapeDtypeStruct((2, norb * 12, 128), bf16),
        in_specs=[pl.BlockSpec(memory_space=pltpu.VMEM), pl.BlockSpec(memory_space=pltpu.VMEM),
                  pl.BlockSpec(memory_space=pl.ANY)],
        out_specs=pl.BlockSpec(memory_space=pltpu.VMEM),
        scratch_shapes=[
            pltpu.VMEM((n_walkers, own_g), bf16),
            pltpu.VMEM((2, 2, n_walkers // 2, 2 * own_g), bf16),
            pltpu.VMEM((2 * own_g, norb, 128), bf16),
            pltpu.VMEM((2, norb // chunks, 2 * own_g, 128), bf16),
            slots, slots, slots, slots,
            dma((2,)), dma((chunks,)), dma((chunks,)), dma((chunks,)), dma((chunks,)), dma((chunks,)),
            dma((chunks, planes)), dma((chunks, planes)), dma((chunks, planes)), dma((chunks, planes)),
            dma((chunks,)), dma((chunks,)),
        ],
        compiler_params=pltpu.CompilerParams(
            collective_id=0, has_side_effects=True, vmem_limit_bytes=58 * 2 ** 20),
        cost_estimate=pl.CostEstimate(
            flops=2 * n_walkers * norb * 256 * own_g, bytes_accessed=norb * own_g * 512, transcendentals=0),
    )(shifted, jnp.asarray(row_orders(planes), bf16), cholesky)


def bias_kernel(planes, rot_ref, trial_ref, chol_ref, aux_ref, out_ref,
                chol, part, half_rot, gathered, turned,
                load_sem, own_sem, z_recv, up_send, down_send, y_send, y_recv, sib_send, sib_recv):
    own_g, norb, _ = chol_ref.shape
    count, nocc, _ = rot_ref.shape
    n_walkers = gathered.shape[0]
    blocks = own_g // 16
    me = lax.axis_index("blk")
    core = lax.rem(me, 2)
    y = lax.rem(lax.div(me, 2), 2)
    z = lax.div(me, 4)
    sibling = me + 1 - 2 * core
    across = me + 2 - 4 * y
    above = me + 4
    below = me - 4
    not_first, not_last = z > 0, z < planes - 1

    def load(b):
        at = pl.ds(b * 16, 16)
        return pltpu.make_async_copy(chol_ref.at[at], chol.at[at], load_sem.at[b])

    for b in range(blocks):
        load(b).start()

    barrier = pltpu.get_barrier_semaphore()
    pl.semaphore_signal(barrier, inc=1, device_id={"blk": sibling}, device_id_type=MESH)
    pl.semaphore_signal(barrier, inc=1, device_id={"blk": across}, device_id_type=MESH)

    @pl.when(not_first)
    def _():
        pl.semaphore_signal(barrier, inc=1, device_id={"blk": below}, device_id_type=MESH)

    @pl.when(not_last)
    def _():
        pl.semaphore_signal(barrier, inc=1, device_id={"blk": above}, device_id_type=MESH)

    peers = 2 + jnp.where(not_first, 1, 0) + jnp.where(not_last, 1, 0)
    pl.semaphore_wait(barrier, peers)

    def move(plane, column, owner_core, send, recv, target):
        piece = gathered.at[pl.ds(((plane * 2 + column) * 2 + owner_core) * count, count)]
        return pltpu.make_async_remote_copy(
            src_ref=piece, dst_ref=piece, send_sem=send, recv_sem=recv,
            device_id={"blk": target}, device_id_type=MESH)

    def go_up(plane):
        return move(plane, y, core, up_send.at[plane], z_recv.at[plane], above)

    def go_down(plane):
        return move(plane, y, core, down_send.at[plane], z_recv.at[plane], below)

    def go_across(plane):
        return move(plane, y, core, y_send.at[plane], y_recv.at[plane], across)

    def from_across(plane):
        return move(plane, 1 - y, core, y_send.at[plane], y_recv.at[plane], across)

    def go_sibling(plane, column):
        return move(plane, column, core, sib_send.at[plane, column], sib_recv.at[plane, column], sibling)

    def from_sibling(plane, column):
        return move(plane, column, 1 - core, sib_send.at[plane, column], sib_recv.at[plane, column], sibling)

    own = pltpu.make_async_copy(rot_ref, gathered.at[pl.ds(me * count, count)], own_sem)
    own.start()
    own.wait()

    @pl.when(not_last)
    def _():
        go_up(z).start()

    @pl.when(not_first)
    def _():
        go_down(z).start()

    go_across(z).start()
    go_sibling(z, y).start()

    def make_half(b):
        load(b).wait()

        def one(j, carry):
            part[j] = jnp.dot(trial_ref[...], chol[b * 16 + j], preferred_element_type=f32).astype(bf16)
            return carry

        lax.fori_loop(0, 16, one, 0)

        def turn(i, carry):
            at = pl.ds(pl.multiple_of(i * 16, 16), 16)
            half_rot[at, pl.ds(b * 16, 16), :] = jnp.swapaxes(part[:, at, :], 0, 1)
            return carry

        lax.fori_loop(0, nocc // 16, turn, 0)

    done = 0
    for t in range(1, planes + 1):
        until = -(-blocks * t // planes)
        for b in range(done, until):
            make_half(b)
        done = until
        if t < planes:
            low, high = z - t, z + t

            @pl.when(low >= 0)
            def _():
                go_up(low).wait_recv()

                @pl.when(not_last)
                def _():
                    go_up(low).start()

                go_across(low).start()
                go_sibling(low, y).start()

            @pl.when(high < planes)
            def _():
                go_down(high).wait_recv()

                @pl.when(not_first)
                def _():
                    go_down(high).start()

                go_across(high).start()
                go_sibling(high, y).start()

        def pass_on(plane):
            from_across(plane).wait_recv()
            go_sibling(plane, 1 - y).start()

        if t == 1:
            pass_on(z)
        else:
            @pl.when(z - (t - 1) >= 0)
            def _():
                pass_on(z - (t - 1))

            @pl.when(z + (t - 1) < planes)
            def _():
                pass_on(z + (t - 1))

    for plane in range(planes):
        for column in range(2):
            from_sibling(plane, column).wait_recv()

    def turn_walkers(w, carry):
        rows = pl.ds(pl.multiple_of(w * 16, 16), 16)

        def turn(i, carry):
            at = pl.ds(pl.multiple_of(i * 16, 16), 16)
            turned[at, rows, :] = jnp.swapaxes(gathered[rows, at, :], 0, 1)
            return carry

        return lax.fori_loop(0, nocc // 16, turn, carry)

    lax.fori_loop(0, n_walkers // 16, turn_walkers, 0)

    def contract(i, total):
        for j in range(4):
            total = total + lax.dot_general(
                turned[i * 4 + j], half_rot[i * 4 + j], (((1,), (1,)), ((), ())),
                preferred_element_type=f32)
        return total

    bias = lax.fori_loop(0, nocc // 4, contract, jnp.zeros((n_walkers, own_g), f32))
    out_ref[...] = (aux_ref[...] + bias_step * bias).astype(bf16)

    for plane in range(planes):
        @pl.when(jnp.logical_and(plane <= z, not_last))
        def _():
            go_up(plane).wait_send()

        @pl.when(jnp.logical_and(plane >= z, not_first))
        def _():
            go_down(plane).wait_send()

        go_across(plane).wait_send()
        for column in range(2):
            go_sibling(plane, column).wait_send()


def shifted_fields(rotated, trial_t, cholesky, aux_fields, planes):
    own_g, norb, _ = cholesky.shape
    nocc = trial_t.shape[0]
    n_walkers = aux_fields.shape[0]
    vmem = pl.BlockSpec(memory_space=pltpu.VMEM)
    dma = pltpu.SemaphoreType.DMA
    return pl.pallas_call(
        functools.partial(bias_kernel, planes),
        out_shape=jax.ShapeDtypeStruct((n_walkers, own_g), bf16),
        in_specs=[vmem, vmem, pl.BlockSpec(memory_space=pl.ANY), vmem],
        out_specs=vmem,
        scratch_shapes=[
            pltpu.VMEM((own_g, norb, norb), bf16),
            pltpu.VMEM((16, nocc, norb), bf16),
            pltpu.VMEM((nocc, own_g, norb), bf16),
            pltpu.VMEM((n_walkers, nocc, norb), bf16),
            pltpu.VMEM((nocc, n_walkers, norb), bf16),
            dma((own_g // 16,)), dma(()), dma((planes,)), dma((planes,)), dma((planes,)),
            dma((planes,)), dma((planes,)), dma((planes, 2)), dma((planes, 2)),
        ],
        compiler_params=pltpu.CompilerParams(
            collective_id=1, has_side_effects=True, vmem_limit_bytes=58 * 2 ** 20),
        cost_estimate=pl.CostEstimate(
            flops=2 * own_g * nocc * norb * (norb + n_walkers),
            bytes_accessed=own_g * norb * norb * 2, transcendentals=0),
    )(rotated, trial_t, cholesky, aux_fields)


def body(planes, walkers, inv_intersection, trial_orbs, cholesky, aux_fields):
    me = lax.axis_index("blk")
    core, z = lax.rem(me, 2), lax.div(me, 4)
    rotated = jnp.einsum(
        "wpi,wij->wjp", walkers, inv_intersection, preferred_element_type=f32
    ).astype(bf16)
    shifted = shifted_fields(rotated, trial_orbs.T, cholesky, aux_fields, planes)
    norb = walkers.shape[1]
    summed = reduced_potential(shifted, cholesky, planes)
    summed = summed.reshape(2, norb // 2, 24, 128)
    straight = summed[:, :, :16].reshape(2, norb, 8, 128)
    mixed = summed[:, :, 16:].reshape(2, norb // 2, 2, 4, 128)
    mixed = jnp.where(lax.rem(z, 2) == 1, mixed[:, :, ::-1], mixed).reshape(2, norb, 4, 128)
    mine = jnp.where(core == 0, straight[:, :, :6],
                     jnp.concatenate([straight[:, :, 6:], mixed], axis=2))
    potential = jnp.transpose((root_step * mine.astype(f32)).astype(bf16), (2, 1, 0, 3))
    potential = potential.reshape(6, norb, norb)
    taylor_term = walkers
    total = walkers.astype(f32)
    for degree in range(1, 5):
        product = jnp.einsum("wpq,wqi->wpi", potential, taylor_term, preferred_element_type=f32)
        taylor_term = (product / degree).astype(bf16)
        total = total + taylor_term.astype(f32)
    new_walkers = total.astype(bf16)
    intersection = jnp.einsum("pi,wpj->wij", trial_orbs, new_walkers, preferred_element_type=f32)
    return (new_walkers, intersection)


def solution(mesh):
    planes = mesh.shape["blk"] // 4
    return jax.shard_map(
        functools.partial(body, planes),
        mesh=mesh,
        in_specs=(
            P(("groups", "blk"), None, None),
            P(("groups", "blk"), None, None),
            P(),
            P(("groups", "blk"), None, None),
            P("groups", "blk"),
        ),
        out_specs=(P(("groups", "blk"), None, None), P(("groups", "blk"), None, None)),
        check_vma=False,
    )
```

```python
import functools

import jax
import jax.numpy as jnp
import numpy as np
from jax import lax
from jax.experimental import pallas as pl
from jax.experimental.pallas import tpu as pltpu
from jax.sharding import PartitionSpec as P

root_step = 0.1
bias_step = 0.5
MESH = pl.DeviceIdType.MESH
bf16 = jnp.bfloat16
f32 = jnp.float32


def row_orders(planes):
    half = planes * 12
    order = np.zeros((2, 2, half), np.int64)
    for parity in range(2):
        for y in range(2):
            for m in range(half):
                if m < planes * 8:
                    dest, within = m // 8, m % 8
                else:
                    rest = m - planes * 8
                    side = (rest % 8) // 4
                    dest = 2 * (rest // 8) + (side if parity == 0 else 1 - side)
                    within = 8 + rest % 4
                order[parity, y, m] = (dest * 2 + y) * 12 + within
    return order.reshape(-1)[:, None] == np.arange(2 * half)[None, :]


def scatter_kernel(planes, chunks, ahead, s_ref, perm_ref, chol_ref, out_ref,
                   sib_s, sp, raw, turned, mine, ysend, held, up, down,
                   s_sem, load_sem, chol_send, chol_recv, y_send, y_recv,
                   up_send, up_recv, down_send, down_recv, out_send, out_recv):
    own_g, norb, _ = chol_ref.shape
    span = norb // chunks
    rows = span * 12
    half = planes * 12
    me = lax.axis_index("blk")
    core = lax.rem(me, 2)
    y = lax.rem(lax.div(me, 2), 2)
    z = lax.div(me, 4)
    sibling = me + 1 - 2 * core
    across = me + 2 - 4 * y
    above = me + 4
    below = me - 4
    not_first, not_last = z > 0, z < planes - 1

    barrier = pltpu.get_barrier_semaphore()
    pl.semaphore_signal(barrier, inc=1, device_id={"blk": sibling}, device_id_type=MESH)
    pl.semaphore_signal(barrier, inc=1, device_id={"blk": across}, device_id_type=MESH)

    @pl.when(not_first)
    def _():
        pl.semaphore_signal(barrier, inc=1, device_id={"blk": below}, device_id_type=MESH)

    @pl.when(not_last)
    def _():
        pl.semaphore_signal(barrier, inc=1, device_id={"blk": above}, device_id_type=MESH)

    peers = 2 + jnp.where(not_first, 1, 0) + jnp.where(not_last, 1, 0)
    pl.semaphore_wait(barrier, peers)

    def remote(src, dst, send, recv, target):
        return pltpu.make_async_remote_copy(
            src_ref=src, dst_ref=dst, send_sem=send, recv_sem=recv,
            device_id={"blk": target}, device_id_type=MESH)

    def chol_load(k):
        return pltpu.make_async_copy(
            chol_ref.at[:, pl.ds(pl.multiple_of(k * span, span), span),
                        pl.ds(pl.multiple_of(core * 128, 128), 128)],
            raw.at[pl.ds(0, own_g), pl.ds(pl.multiple_of(k * span, span), span)], load_sem.at[k])

    def chol_swap(k):
        return remote(
            chol_ref.at[:, pl.ds(pl.multiple_of(k * span, span), span),
                        pl.ds(pl.multiple_of((1 - core) * 128, 128), 128)],
            raw.at[pl.ds(own_g, own_g), pl.ds(pl.multiple_of(k * span, span), span)],
            chol_send.at[k], chol_recv.at[k], sibling)

    def y_copy(k):
        return remote(ysend.at[k], held.at[k], y_send.at[k], y_recv.at[k], across)

    def out_copy(k):
        piece = out_ref.at[core, pl.ds(pl.multiple_of(k * rows, 16), rows)]
        return remote(piece, piece, out_send.at[k], out_recv.at[k], sibling)

    s_copy = remote(s_ref, sib_s, s_sem.at[0], s_sem.at[1], sibling)
    s_copy.start()

    def begin(k, carry):
        chol_load(k).start()
        chol_swap(k).start()
        return carry

    lax.fori_loop(0, ahead, begin, 0)
    s_copy.wait()
    for parity in range(2):
        for place, side in ((0, 1 - y), (1, y)):
            pick = perm_ref[pl.ds(pl.multiple_of((parity * 2 + side) * half, 16), half), :]
            at = pl.ds(place * half, half)
            sp[parity, at, 0:own_g] = jnp.dot(
                pick, s_ref[...], preferred_element_type=f32).astype(bf16)
            sp[parity, at, own_g:] = jnp.dot(
                pick, sib_s[...], preferred_element_type=f32).astype(bf16)

    low = lax.broadcasted_iota(jnp.int32, (8, 128), 0) < 4

    def products(k):
        slot = lax.rem(k, 2)

        def quad(j, carry):
            r = [jnp.dot(sp[i % 2], turned[slot, j * 4 + i], preferred_element_type=f32)
                 for i in range(4)]
            at = pl.ds(pl.multiple_of(j * 48, 48), 48)
            for place in range(2):
                base = place * half
                for d in range(planes):
                    pieces = []
                    start, rest = base + d * 8, base + planes * 8 + (d // 2) * 8
                    for i in (0, 2):
                        even, odd = r[i][rest:rest + 8], r[i + 1][rest:rest + 8]
                        pieces += [r[i][start:start + 8], r[i + 1][start:start + 8],
                                   jnp.where(low, even, odd) if d % 2 == 0 else jnp.where(low, odd, even)]
                    value = jnp.concatenate(pieces, axis=0).astype(bf16)
                    if place == 0:
                        ysend[k, d, at] = value
                    else:
                        mine[slot, d, at] = value
            return carry

        lax.fori_loop(0, span // 4, quad, 0, unroll=2)

    def hop(k, d, buf, send, recv, has_source, target):
        @pl.when(has_source)
        def _():
            remote(buf.at[k, d], buf.at[k, d], send.at[k, d], recv.at[k, d], target).wait_recv()
            buf[k, d] = (buf[k, d].astype(f32) + held[k, d].astype(f32)).astype(bf16)
            remote(buf.at[k, d], buf.at[k, d], send.at[k, d], recv.at[k, d], target).start()

        @pl.when(jnp.logical_not(has_source))
        def _():
            remote(held.at[k, d], buf.at[k, d], send.at[k, d], recv.at[k, d], target).start()

    def step(t, carry):
        @pl.when(t + ahead < chunks)
        def _():
            begin(t + ahead, 0)

        @pl.when(t < chunks)
        def _():
            chol_load(t).wait()
            chol_swap(t).wait_recv()
            columns = pl.ds(pl.multiple_of(t * span, span), span)

            def turn(b, carry):
                at = pl.ds(pl.multiple_of(b * 16, 16), 16)
                turned[lax.rem(t, 2), :, at, :] = jnp.swapaxes(raw[at, columns, :], 0, 1)
                return carry

            lax.fori_loop(0, 2 * own_g // 16, turn, 0)
            products(t)
            y_copy(t).start()

        @pl.when(jnp.logical_and(t >= 1, t <= chunks))
        def _():
            k = t - 1
            y_copy(k).wait_recv()
            slot = lax.rem(k, 2)
            for d in range(planes):
                held[k, d] = (held[k, d].astype(f32) + mine[slot, d].astype(f32)).astype(bf16)

        ku = t - 1 - z

        @pl.when(jnp.logical_and(ku >= 0, ku < chunks))
        def _():
            for d in range(1, planes):
                @pl.when(d > z)
                def _():
                    hop(ku, d, up, up_send, up_recv, not_first, above)

        kd = t - planes + z

        @pl.when(jnp.logical_and(kd >= 0, kd < chunks))
        def _():
            for d in range(planes - 1):
                @pl.when(d < z)
                def _():
                    hop(kd, d, down, down_send, down_recv, not_last, below)

        kf = t - planes

        @pl.when(jnp.logical_and(kf >= 0, kf < chunks))
        def _():
            at = pl.ds(pl.multiple_of(kf * rows, 16), rows)

            @pl.when(jnp.logical_not(not_first))
            def _():
                remote(down.at[kf, z], down.at[kf, z], down_send.at[kf, z], down_recv.at[kf, z], above).wait_recv()
                out_ref[core, at] = (held[kf, z].astype(f32) + down[kf, z].astype(f32)).astype(bf16)

            @pl.when(jnp.logical_not(not_last))
            def _():
                remote(up.at[kf, z], up.at[kf, z], up_send.at[kf, z], up_recv.at[kf, z], below).wait_recv()
                out_ref[core, at] = (held[kf, z].astype(f32) + up[kf, z].astype(f32)).astype(bf16)

            @pl.when(jnp.logical_and(not_first, not_last))
            def _():
                remote(down.at[kf, z], down.at[kf, z], down_send.at[kf, z], down_recv.at[kf, z], above).wait_recv()
                remote(up.at[kf, z], up.at[kf, z], up_send.at[kf, z], up_recv.at[kf, z], below).wait_recv()
                out_ref[core, at] = (
                    held[kf, z].astype(f32) + up[kf, z].astype(f32) + down[kf, z].astype(f32)
                ).astype(bf16)

            out_copy(kf).start()

        return carry

    lax.fori_loop(0, chunks + planes, step, 0)

    def finish(k, carry):
        chol_swap(k).wait_send()
        y_copy(k).wait_send()
        for d in range(planes):
            @pl.when(d > z)
            def _():
                remote(up.at[k, d], up.at[k, d], up_send.at[k, d], up_recv.at[k, d], above).wait_send()

            @pl.when(d < z)
            def _():
                remote(down.at[k, d], down.at[k, d], down_send.at[k, d], down_recv.at[k, d], below).wait_send()

        out_copy(k).wait_send()
        other = out_ref.at[1 - core, pl.ds(pl.multiple_of(k * rows, 16), rows)]
        remote(other, other, out_send.at[k], out_recv.at[k], sibling).wait_recv()
        return carry

    lax.fori_loop(0, chunks, finish, 0)


def reduced_potential(shifted, cholesky, planes, chunks=16):
    n_walkers, own_g = shifted.shape
    norb = cholesky.shape[1]
    rows = norb // chunks * 12
    slots = pltpu.VMEM((chunks, planes, rows, 128), bf16)
    dma = pltpu.SemaphoreType.DMA
    return pl.pallas_call(
        functools.partial(scatter_kernel, planes, chunks, 3),
        out_shape=jax.ShapeDtypeStruct((2, norb * 12, 128), bf16),
        in_specs=[pl.BlockSpec(memory_space=pltpu.VMEM), pl.BlockSpec(memory_space=pltpu.VMEM),
                  pl.BlockSpec(memory_space=pl.ANY)],
        out_specs=pl.BlockSpec(memory_space=pltpu.VMEM),
        scratch_shapes=[
            pltpu.VMEM((n_walkers, own_g), bf16),
            pltpu.VMEM((2, n_walkers, 2 * own_g), bf16),
            pltpu.VMEM((2 * own_g, norb, 128), bf16),
            pltpu.VMEM((2, norb // chunks, 2 * own_g, 128), bf16),
            pltpu.VMEM((2, planes, rows, 128), bf16),
            slots, slots, slots, slots,
            dma((2,)), dma((chunks,)), dma((chunks,)), dma((chunks,)), dma((chunks,)), dma((chunks,)),
            dma((chunks, planes)), dma((chunks, planes)), dma((chunks, planes)), dma((chunks, planes)),
            dma((chunks,)), dma((chunks,)),
        ],
        compiler_params=pltpu.CompilerParams(
            collective_id=0, has_side_effects=True, vmem_limit_bytes=58 * 2 ** 20),
        cost_estimate=pl.CostEstimate(
            flops=2 * n_walkers * norb * 256 * own_g, bytes_accessed=norb * own_g * 512, transcendentals=0),
    )(shifted, jnp.asarray(row_orders(planes), bf16), cholesky)


def bias_kernel(planes, rot_ref, trial_ref, chol_ref, aux_ref, out_ref,
                chol, part, half_rot, gathered, turned,
                load_sem, own_sem, z_recv, up_send, down_send, y_send, y_recv, sib_send, sib_recv):
    own_g, norb, _ = chol_ref.shape
    count, nocc, _ = rot_ref.shape
    n_walkers = gathered.shape[0]
    blocks = own_g // 16
    me = lax.axis_index("blk")
    core = lax.rem(me, 2)
    y = lax.rem(lax.div(me, 2), 2)
    z = lax.div(me, 4)
    sibling = me + 1 - 2 * core
    across = me + 2 - 4 * y
    above = me + 4
    below = me - 4
    not_first, not_last = z > 0, z < planes - 1

    def load(b):
        at = pl.ds(b * 16, 16)
        return pltpu.make_async_copy(chol_ref.at[at], chol.at[at], load_sem.at[b])

    for b in range(blocks):
        load(b).start()

    barrier = pltpu.get_barrier_semaphore()
    pl.semaphore_signal(barrier, inc=1, device_id={"blk": sibling}, device_id_type=MESH)
    pl.semaphore_signal(barrier, inc=1, device_id={"blk": across}, device_id_type=MESH)

    @pl.when(not_first)
    def _():
        pl.semaphore_signal(barrier, inc=1, device_id={"blk": below}, device_id_type=MESH)

    @pl.when(not_last)
    def _():
        pl.semaphore_signal(barrier, inc=1, device_id={"blk": above}, device_id_type=MESH)

    peers = 2 + jnp.where(not_first, 1, 0) + jnp.where(not_last, 1, 0)
    pl.semaphore_wait(barrier, peers)

    def move(plane, column, owner_core, send, recv, target):
        piece = gathered.at[pl.ds(((plane * 2 + column) * 2 + owner_core) * count, count)]
        return pltpu.make_async_remote_copy(
            src_ref=piece, dst_ref=piece, send_sem=send, recv_sem=recv,
            device_id={"blk": target}, device_id_type=MESH)

    def go_up(plane):
        return move(plane, y, core, up_send.at[plane], z_recv.at[plane], above)

    def go_down(plane):
        return move(plane, y, core, down_send.at[plane], z_recv.at[plane], below)

    def go_across(plane):
        return move(plane, y, core, y_send.at[plane], y_recv.at[plane], across)

    def from_across(plane):
        return move(plane, 1 - y, core, y_send.at[plane], y_recv.at[plane], across)

    def go_sibling(plane, column):
        return move(plane, column, core, sib_send.at[plane, column], sib_recv.at[plane, column], sibling)

    def from_sibling(plane, column):
        return move(plane, column, 1 - core, sib_send.at[plane, column], sib_recv.at[plane, column], sibling)

    own = pltpu.make_async_copy(rot_ref, gathered.at[pl.ds(me * count, count)], own_sem)
    own.start()
    own.wait()

    @pl.when(not_last)
    def _():
        go_up(z).start()

    @pl.when(not_first)
    def _():
        go_down(z).start()

    go_across(z).start()
    go_sibling(z, y).start()

    def make_half(b):
        load(b).wait()

        def one(j, carry):
            part[j] = jnp.dot(trial_ref[...], chol[b * 16 + j], preferred_element_type=f32).astype(bf16)
            return carry

        lax.fori_loop(0, 16, one, 0)

        def turn(i, carry):
            at = pl.ds(pl.multiple_of(i * 16, 16), 16)
            half_rot[at, pl.ds(b * 16, 16), :] = jnp.swapaxes(part[:, at, :], 0, 1)
            return carry

        lax.fori_loop(0, nocc // 16, turn, 0)

    done = 0
    for t in range(1, planes + 1):
        until = -(-blocks * t // planes)
        for b in range(done, until):
            make_half(b)
        done = until
        if t < planes:
            low, high = z - t, z + t

            @pl.when(low >= 0)
            def _():
                go_up(low).wait_recv()

                @pl.when(not_last)
                def _():
                    go_up(low).start()

                go_across(low).start()
                go_sibling(low, y).start()

            @pl.when(high < planes)
            def _():
                go_down(high).wait_recv()

                @pl.when(not_first)
                def _():
                    go_down(high).start()

                go_across(high).start()
                go_sibling(high, y).start()

        def pass_on(plane):
            from_across(plane).wait_recv()
            go_sibling(plane, 1 - y).start()

        if t == 1:
            pass_on(z)
        else:
            @pl.when(z - (t - 1) >= 0)
            def _():
                pass_on(z - (t - 1))

            @pl.when(z + (t - 1) < planes)
            def _():
                pass_on(z + (t - 1))

    for plane in range(planes):
        for column in range(2):
            from_sibling(plane, column).wait_recv()

    def turn_walkers(w, carry):
        rows = pl.ds(pl.multiple_of(w * 16, 16), 16)

        def turn(i, carry):
            at = pl.ds(pl.multiple_of(i * 16, 16), 16)
            turned[at, rows, :] = jnp.swapaxes(gathered[rows, at, :], 0, 1)
            return carry

        return lax.fori_loop(0, nocc // 16, turn, carry)

    lax.fori_loop(0, n_walkers // 16, turn_walkers, 0)

    def contract(i, total):
        for j in range(4):
            total = total + lax.dot_general(
                turned[i * 4 + j], half_rot[i * 4 + j], (((1,), (1,)), ((), ())),
                preferred_element_type=f32)
        return total

    bias = lax.fori_loop(0, nocc // 4, contract, jnp.zeros((n_walkers, own_g), f32))
    out_ref[...] = (aux_ref[...] + bias_step * bias).astype(bf16)

    for plane in range(planes):
        @pl.when(jnp.logical_and(plane <= z, not_last))
        def _():
            go_up(plane).wait_send()

        @pl.when(jnp.logical_and(plane >= z, not_first))
        def _():
            go_down(plane).wait_send()

        go_across(plane).wait_send()
        for column in range(2):
            go_sibling(plane, column).wait_send()


def shifted_fields(rotated, trial_t, cholesky, aux_fields, planes):
    own_g, norb, _ = cholesky.shape
    nocc = trial_t.shape[0]
    n_walkers = aux_fields.shape[0]
    vmem = pl.BlockSpec(memory_space=pltpu.VMEM)
    dma = pltpu.SemaphoreType.DMA
    return pl.pallas_call(
        functools.partial(bias_kernel, planes),
        out_shape=jax.ShapeDtypeStruct((n_walkers, own_g), bf16),
        in_specs=[vmem, vmem, pl.BlockSpec(memory_space=pl.ANY), vmem],
        out_specs=vmem,
        scratch_shapes=[
            pltpu.VMEM((own_g, norb, norb), bf16),
            pltpu.VMEM((16, nocc, norb), bf16),
            pltpu.VMEM((nocc, own_g, norb), bf16),
            pltpu.VMEM((n_walkers, nocc, norb), bf16),
            pltpu.VMEM((nocc, n_walkers, norb), bf16),
            dma((own_g // 16,)), dma(()), dma((planes,)), dma((planes,)), dma((planes,)),
            dma((planes,)), dma((planes,)), dma((planes, 2)), dma((planes, 2)),
        ],
        compiler_params=pltpu.CompilerParams(
            collective_id=1, has_side_effects=True, vmem_limit_bytes=58 * 2 ** 20),
        cost_estimate=pl.CostEstimate(
            flops=2 * own_g * nocc * norb * (norb + n_walkers),
            bytes_accessed=own_g * norb * norb * 2, transcendentals=0),
    )(rotated, trial_t, cholesky, aux_fields)


def body(planes, walkers, inv_intersection, trial_orbs, cholesky, aux_fields):
    me = lax.axis_index("blk")
    core, z = lax.rem(me, 2), lax.div(me, 4)
    rotated = jnp.einsum(
        "wpi,wij->wjp", walkers, inv_intersection, preferred_element_type=f32
    ).astype(bf16)
    shifted = shifted_fields(rotated, trial_orbs.T, cholesky, aux_fields, planes)
    norb = walkers.shape[1]
    summed = reduced_potential(shifted, cholesky, planes)
    summed = summed.reshape(2, norb // 2, 24, 128)
    straight = summed[:, :, :16].reshape(2, norb, 8, 128)
    mixed = summed[:, :, 16:].reshape(2, norb // 2, 2, 4, 128)
    mixed = jnp.where(lax.rem(z, 2) == 1, mixed[:, :, ::-1], mixed).reshape(2, norb, 4, 128)
    mine = jnp.where(core == 0, straight[:, :, :6],
                     jnp.concatenate([straight[:, :, 6:], mixed], axis=2))
    potential = jnp.transpose((root_step * mine.astype(f32)).astype(bf16), (2, 1, 0, 3))
    potential = potential.reshape(6, norb, norb)
    taylor_term = walkers
    total = walkers.astype(f32)
    for degree in range(1, 5):
        product = jnp.einsum("wpq,wqi->wpi", potential, taylor_term, preferred_element_type=f32)
        taylor_term = (product / degree).astype(bf16)
        total = total + taylor_term.astype(f32)
    new_walkers = total.astype(bf16)
    intersection = jnp.einsum("pi,wpj->wij", trial_orbs, new_walkers, preferred_element_type=f32)
    return (new_walkers, intersection)


def solution(mesh):
    planes = mesh.shape["blk"] // 4
    return jax.shard_map(
        functools.partial(body, planes),
        mesh=mesh,
        in_specs=(
            P(("groups", "blk"), None, None),
            P(("groups", "blk"), None, None),
            P(),
            P(("groups", "blk"), None, None),
            P("groups", "blk"),
        ),
        out_specs=(P(("groups", "blk"), None, None), P(("groups", "blk"), None, None)),
        check_vma=False,
    )
```
